32 devices in a mesh: region: 2 (over x), graph: 16 (over z, y, core).
Axes of the slice: x: 2, y: 2, z: 4, core: 2. Of those that a mesh axis runs over, the one named last changes fastest.
Arguments:
- observed: float32 [96, 256, 128], P(None, ('region', 'graph')), parts along dimension 1, may hold values from -6 to 6
- mask: int32 [96, 256, 128], P(None, ('region', 'graph')), parts along dimension 1, may hold values 0 or 1
- first_guess: float32 [96, 256, 128], P(None, ('region', 'graph')), parts along dimension 1, may hold values from -4 to 4
- diag_weight: float32 [256, 128], P(('region', 'graph')), parts along dimension 0, may hold values from 0.2 to 2
- coupling: bfloat16 [256, 5, 128, 128], P(('region', 'graph')), parts along dimension 0, may hold values from 0 to 0.0015563965
- block_cols: int32 [256, 5], P(('region', 'graph')), parts along dimension 0, may hold values from 0 to 23, as said below
- send_rows: int32 [32, 4, 4], P(('region', 'graph')), parts along dimension 0, may hold values from 0 to 7, as said below
Outputs:
- solution_field: float32 [96, 256, 128], P(None, ('region', 'graph')), parts along dimension 1
- residual: float32 [96, 256, 128], P(None, ('region', 'graph')), parts along dimension 1
The draws below stay inside these ranges and needn't reach their ends.
There are 2 independent parts, one for each index of `region`. The reference program is written for one: setup_inputs(seed, part) draws one part's arguments, and reference() takes and returns one part's arrays. A program takes and returns all parts, laid end to end along the dimension named above; each array names one. Nothing has to cross between parts.
Inputs may be any that keep to these rules, and one draw needn't show every extreme that they name: `block_cols`: slot 0 of block row i is the row's own block i modulo 8; the other slots are any of the 24 extended blocks. `send_rows`: the 4 entries of one partition and offset are distinct own blocks.
All inputs are finite; a program needn't handle non-finite values. No bound on the sum of `mask` on one device may be relied on, other than what follows from the above.
Results may differ from the reference program's by a relative error of at most 0.0003.
Values sent between devices are 32-bit elements; how exact they have to be, the bound alone decides.
A program may use at most 64 MiB of HBM per device.

```python
import math
import jax
import jax.numpy as jnp
from jax import lax

BLK = 128
STEPS = 96
BLK_DEV = 8
NB = 5
CAP = 4
ITERS = 2
BLOCKS = 128
EXT = 24
N_GRAPH = 16


def draw_block_cols(key, part):
    key = jax.random.fold_in(key, 11)
    far_ids = jax.random.randint(key, (BLOCKS, NB - 1), 0, EXT)
    far_ids = far_ids.at[0, 0].set(EXT - 1)
    home_ids = (jnp.arange(BLOCKS) % BLK_DEV)[:, None]
    return jnp.concatenate([home_ids, far_ids], axis=1).astype(jnp.int32)


def draw_send_rows(key, part):
    key = jax.random.fold_in(key, 23)
    scores = jax.random.randint(key, (N_GRAPH, 4, BLK_DEV), 0, 2 ** 20) * BLK_DEV + jnp.arange(BLK_DEV)[None, None, :]
    ordered = jnp.argsort(scores, axis=-1)
    return ordered[:, :, :CAP].astype(jnp.int32)


def set_ends(entries, key, low, top_value):
    extent = entries.shape
    place = [jax.random.randint(jax.random.fold_in(key, axis), (), 0, extent[axis]) for axis in range(len(extent))]
    entries = entries.at[tuple(place)].set(low)
    longest = extent.index(max(extent))
    place[longest] = (place[longest] + 1) % extent[longest]
    return entries.at[tuple(place)].set(top_value)


def block_levels(own_key, shape, split, low, high):
    level, own = 1.0, jax.random.fold_in(own_key, 6)
    for dim, blocks in split:
        steps = jnp.exp(jax.random.uniform(jax.random.fold_in(own, dim), (blocks,), jnp.float32, low / len(split), high / len(split)))
        level = level * jnp.repeat(steps, shape[dim] // blocks).reshape([-1 if axis == dim else 1 for axis in range(len(shape))])
    return level


def centred(key, shape, scale, bound, split=(), kind=jnp.bfloat16):
    entries = scale * jax.random.normal(key, shape, jnp.float32)
    if split:
        entries = entries * block_levels(key, shape, split, -0.22, 0.18)
    return jnp.clip(entries, -bound, bound).astype(kind)


def setup_inputs(seed: int = 0, part: int = 0) -> dict:
    splits = jax.random.split(jax.random.key(seed), 8)
    part_keys = jax.random.split(jax.random.fold_in(splits[7], part), 8)
    return {
        "observed": centred(part_keys[0], (STEPS, BLOCKS, BLK), 1.0, 6.0, ((1, 16),), jnp.float32),
        "mask": set_ends((jax.random.randint(part_keys[1], (STEPS, BLOCKS, BLK), 0, 5) < 2).astype(jnp.int32), jax.random.fold_in(part_keys[1], 1), 0, 1),
        "first_guess": centred(part_keys[2], (STEPS, BLOCKS, BLK), 0.5, 4.0, ((1, 16),), jnp.float32),
        "diag_weight": jnp.clip(jnp.exp(math.log(2.0) - 2.3025851 * jax.random.uniform(part_keys[3], (BLOCKS, BLK), jnp.float32) ** block_levels(part_keys[3], (BLOCKS, BLK), ((0, 16),), -0.2, 0.2)), 0.2, 2.0),
        "coupling": jnp.clip(0.0015563965 * jax.random.uniform(part_keys[4], (BLOCKS, NB, BLK, BLK), jnp.float32) ** block_levels(part_keys[4], (BLOCKS, NB, BLK, BLK), ((0, 16),), -0.2, 0.2), 0.0, 0.0015563965).astype(jnp.bfloat16),
        "block_cols": draw_block_cols(jax.random.fold_in(jax.random.fold_in(splits[7], part), 71), part),
        "send_rows": draw_send_rows(jax.random.fold_in(jax.random.fold_in(splits[7], part), 71), part),
    }


OFFSETS = (1, -1, 2, -2)
time_tie = 0.5
highest = lax.Precision.HIGHEST


def by_partition(field):
    return field.reshape(field.shape[0], N_GRAPH, BLK_DEV, BLK).transpose(1, 0, 2, 3)


def joined(parts):
    return parts.transpose(1, 0, 2, 3).reshape(parts.shape[1], N_GRAPH * BLK_DEV, BLK)


def shift_parts(stack, offset):
    blank = jnp.zeros((abs(offset),) + stack.shape[1:], stack.dtype)
    if offset > 0:
        return jnp.concatenate([blank, stack[:-offset]], axis=0)
    return jnp.concatenate([stack[-offset:], blank], axis=0)


def pick_rows(parts, rows):
    return jax.vmap(lambda field, chosen: field[:, chosen])(parts, rows)


def forward_all(parts, weights, column_ids, send_rows):
    arrived = [shift_parts(pick_rows(parts, send_rows[:, index]), offset) for index, offset in enumerate(OFFSETS)]
    extended = jnp.concatenate([parts] + arrived, axis=2)

    def single(items):
        field, block_w, ids = items
        gathered = jnp.take(field, ids.reshape(-1), axis=1).reshape(field.shape[0], BLK_DEV, NB, BLK)
        return jnp.einsum('bkrc,tbkc->tbr', block_w.astype(jnp.float32), gathered, precision=highest)

    return lax.map(single, (extended, weights, column_ids))


def transpose_all(parts, weights, column_ids, send_rows):
    count = parts.shape[1]

    def single(items):
        field, block_w, ids = items
        terms = jnp.einsum('bkrc,tbr->tbkc', block_w.astype(jnp.float32), field, precision=highest)
        terms = terms.reshape(count, BLK_DEV * NB, BLK)
        return jnp.zeros((count, EXT, BLK), jnp.float32).at[:, ids.reshape(-1)].add(terms)

    collected = lax.map(single, (parts, weights, column_ids))
    total = collected[:, :, :BLK_DEV]
    for index, offset in enumerate(OFFSETS):
        piece = collected[:, :, BLK_DEV + index * CAP:BLK_DEV + (index + 1) * CAP]
        back = shift_parts(piece, -offset)
        total = jax.vmap(lambda whole, chosen, extra: whole.at[:, chosen].add(extra))(total, send_rows[:, index], back)
    return total


def time_laplace(field):
    before = jnp.concatenate([field[:1], field[:-1]], axis=0)
    after = jnp.concatenate([field[1:], field[-1:]], axis=0)
    return 2.0 * field - before - after


def reference(observed, mask, first_guess, diag_weight, coupling, block_cols, send_rows):
    weights = coupling.reshape(N_GRAPH, BLK_DEV, NB, BLK, BLK)
    column_ids = block_cols.reshape(N_GRAPH, BLK_DEV, NB)
    unit_field = jnp.ones((1, N_GRAPH * BLK_DEV, BLK), jnp.float32)
    row_part = jnp.sum(weights.astype(jnp.float32), axis=(2, 4))
    column_part = transpose_all(by_partition(unit_field), weights, column_ids, send_rows)[:, 0]
    degree = (row_part + column_part).reshape(N_GRAPH * BLK_DEV, BLK)
    mask_f = mask.astype(jnp.float32)
    diagonal = mask_f + diag_weight[None] + degree[None]

    def operate(field):
        parts = by_partition(field)
        coupled = forward_all(parts, weights, column_ids, send_rows) + transpose_all(parts, weights, column_ids, send_rows)
        return diagonal * field - joined(coupled) + time_tie * time_laplace(field)

    right_side = mask_f * observed
    solution_field = first_guess
    residual = right_side - operate(first_guess)
    direction = residual
    norm_now = jnp.sum(residual * residual)
    for step in range(ITERS):
        image = operate(direction)
        step_size = norm_now / jnp.sum(direction * image)
        solution_field = solution_field + step_size * direction
        residual = residual - step_size * image
        norm_next = jnp.sum(residual * residual)
        direction = residual + (norm_next / norm_now) * direction
        norm_now = norm_next
    return solution_field, residual
```

```python
import functools

import jax
import jax.numpy as jnp
from jax import lax
from jax.experimental import pallas as pl
from jax.experimental.pallas import tpu as pltpu
from jax.sharding import PartitionSpec as P

ITERS = 2
APPLIED = ITERS + 1
OFFSETS = (1, -1, 2, -2)
time_tie = 0.5
CHUNKS = 2
MESH = pl.DeviceIdType.MESH
OWN, PAIR, FACE, FAR, SIDE = range(5)


def shifted(block, axis, distance):
    devices = range(lax.axis_size(axis))
    route = [(i - distance, i) for i in devices if i - distance in devices]
    return lax.ppermute(block, axis, route)


def split_parts(field):
    upper = field.astype(jnp.bfloat16)
    lower = (field - upper.astype(jnp.float32)).astype(jnp.bfloat16)
    return [upper, lower]


def fold_rows(values):
    total = values[0:8]
    for start in range(8, values.shape[0], 8):
        total = total + values[start : start + 8]
    return total


def total_of(tile):
    return jnp.sum(jnp.sum(tile, axis=0, keepdims=True), axis=1, keepdims=True)


def cg_kernel(
    count,
    blocks,
    slots,
    steps,
    places_ref,
    before_ref,
    last_ref,
    observed_ref,
    mask_ref,
    guess_ref,
    prior_ref,
    weights_ref,
    solution_ref,
    residual_ref,
    *scratch,
):
    ext = [scratch[s * CHUNKS : (s + 1) * CHUNKS] for s in range(APPLIED)]
    final, mask_f, right, sums, kept, out_terms, in_terms, diag, red_out, red_in = scratch[APPLIED * CHUNKS : -4]
    send_sem, recv_sem, red_send_sem, red_recv_sem = scratch[-4:]
    width = guess_ref.shape[2]
    me = lax.axis_index("graph")
    core = lax.rem(me, 2)
    face = lax.rem(me // 2, 2)
    pair_id = me + 1 - 2 * core
    face_id = me + 2 - 4 * face
    far_src = me - 4 + 8 * face
    far_dst = me + 4 - 8 * face
    has_src = (far_src >= 0) & (far_src < count)
    has_dst = (far_dst >= 0) & (far_dst < count)
    same = core == face
    always = me >= 0
    part = steps // CHUNKS
    terms = blocks * slots
    f32 = jnp.float32

    barrier = pltpu.get_barrier_semaphore()
    for step in range(1, count):
        pl.semaphore_signal(barrier, inc=1, device_id={"graph": lax.rem(me + step, count)}, device_id_type=MESH)

    for i in range(blocks):
        for chunk in range(CHUNKS):
            ext[0][chunk][i] = guess_ref[chunk * part : (chunk + 1) * part, i, :]

    @pl.when(jnp.logical_not(has_src))
    def _():
        for held in scratch[: APPLIED * CHUNKS]:
            held[FAR * blocks : (FAR + 1) * blocks] = jnp.zeros((blocks, part, width), f32)

    @pl.when(same & jnp.logical_not(has_src))
    def _():
        for held in scratch[: APPLIED * CHUNKS]:
            held[SIDE * blocks : (SIDE + 1) * blocks] = jnp.zeros((blocks, part, width), f32)

    sums[terms] = jnp.zeros(sums.shape[1:], f32)
    pl.semaphore_wait(barrier, count - 1)

    pending = []

    def field_copy(s, chunk, kind, src_role, dst_role, target):
        return pltpu.make_async_remote_copy(
            src_ref=ext[s][chunk].at[pl.ds(src_role * blocks, blocks)],
            dst_ref=ext[s][chunk].at[pl.ds(dst_role * blocks, blocks)],
            send_sem=send_sem.at[s, chunk, kind],
            recv_sem=recv_sem.at[s, chunk, kind],
            device_id={"graph": target},
            device_id_type=MESH,
        )

    def term_rows(s, chunk):
        if s == 0 and chunk == 0:
            return 0, part + 8
        return 8 + chunk * part, part

    def term_copy(s, chunk, role, target):
        start, size = term_rows(s, chunk)
        return pltpu.make_async_remote_copy(
            src_ref=out_terms.at[s, pl.ds((role - 1) * blocks, blocks), pl.ds(start, size)],
            dst_ref=in_terms.at[s, pl.ds((role - 1) * blocks, blocks), pl.ds(start, size)],
            send_sem=send_sem.at[s, chunk, 3 + role],
            recv_sem=recv_sem.at[s, chunk, 3 + role],
            device_id={"graph": target},
            device_id_type=MESH,
        )

    def start(cond, make):
        copy = make()
        pl.when(cond)(copy.start)
        pending.append((cond, copy))

    def arrived(cond, make):
        pl.when(cond)(make().wait_recv)

    def copies(s, chunk):
        field = {
            PAIR: lambda: field_copy(s, chunk, 0, OWN, PAIR, pair_id),
            FACE: lambda: field_copy(s, chunk, 1, OWN, FACE, face_id),
            FAR: lambda: field_copy(s, chunk, 2, FACE, FAR, far_dst),
            SIDE: lambda: field_copy(s, chunk, 3, FACE, SIDE, pair_id),
            "other": lambda: field_copy(s, chunk, 3, FAR, SIDE, pair_id),
        }
        term = {
            PAIR: lambda: term_copy(s, chunk, PAIR, pair_id),
            FACE: lambda: term_copy(s, chunk, FACE, face_id),
            FAR: lambda: term_copy(s, chunk, FAR, far_src),
            SIDE: lambda: term_copy(s, chunk, SIDE, pair_id),
        }
        return field, term

    def add_terms(s, chunk, role, other):
        start_row, size = term_rows(s, chunk)
        rows = pl.ds(start_row, size)

        def body(j, carry):
            at = (role - 1) * blocks + j
            out_terms[s, at, rows] = out_terms[s, at, rows] + in_terms[s, (other - 1) * blocks + j, rows]
            return carry

        lax.fori_loop(0, blocks, body, 0)

    def send_stage(s, chunk):
        field, term = copies(s, chunk)
        start(always, field[FACE])
        start(always, field[PAIR])
        start_row, size = term_rows(s, chunk)
        with_ones = size > part
        rows = pl.ds(start_row, size)

        def row_body(i, carry):
            own = ext[s][chunk][i]
            pieces = split_parts(own)
            if with_ones:
                pieces.append(jnp.ones((16, own.shape[1]), jnp.bfloat16))
            stacked = jnp.concatenate(pieces, axis=0)
            for k in range(slots):
                made = jnp.dot(stacked, weights_ref[i, k], preferred_element_type=f32)
                term_now = made[:part] + made[part : 2 * part]
                if with_ones:
                    term_now = jnp.concatenate([made[2 * part : 2 * part + 8], term_now], axis=0)
                at = i * slots + k
                sums[at, :size] = term_now + sums[before_ref[at], :size]
            return carry

        lax.fori_loop(0, blocks, row_body, 0)
        for role in (SIDE, FAR, PAIR, FACE):

            def pick(j, carry, role=role):
                out_terms[s, (role - 1) * blocks + j, rows] = sums[last_ref[role * blocks + j], :size]
                return carry

            lax.fori_loop(0, blocks, pick, 0)
            if role == SIDE:
                start(jnp.logical_not(same) | has_src, term[SIDE])
            if role == FAR:
                start(same & has_src, term[FAR])
            if role == PAIR:
                start(always, term[PAIR])

        def keep(j, carry):
            kept[s, j, rows] = sums[last_ref[j], :size]
            return carry

        lax.fori_loop(0, blocks, keep, 0)

    def far_terms_stage(s, chunk):
        field, term = copies(s, chunk)
        moved = jnp.logical_not(same) & has_src
        arrived(same | has_src, term[SIDE])

        @pl.when(moved)
        def _():
            add_terms(s, chunk, FAR, SIDE)

        start(moved, term[FAR])

    def face_relay_stage(s, chunk):
        field, term = copies(s, chunk)
        arrived(always, field[FACE])
        start(has_dst, field[FAR])
        start(same, field[SIDE])

    def face_terms_stage(s, chunk):
        field, term = copies(s, chunk)

        @pl.when(same)
        def _():
            add_terms(s, chunk, FACE, SIDE)

        arrived(has_dst, term[FAR])

        @pl.when(has_dst)
        def _():
            add_terms(s, chunk, FACE, FAR)

        start(always, term[FACE])

    def far_relay_stage(s, chunk):
        field, term = copies(s, chunk)
        arrived(has_src, field[FAR])
        start(jnp.logical_not(same) & has_src, field["other"])

    def finish_stage(s, chunk):
        field, term = copies(s, chunk)
        start_row, size = term_rows(s, chunk)
        with_ones = size > part
        here = pl.ds(chunk * part, part)
        arrived(always, field[PAIR])
        arrived(jnp.logical_not(same) | has_src, field[SIDE])
        arrived(always, term[PAIR])
        arrived(always, term[FACE])

        def row_body(i, carry):
            made = None
            for k in range(slots):
                pieces = split_parts(ext[s][chunk][places_ref[i * slots + k]])
                if with_ones:
                    pieces.append(jnp.ones((16, width), jnp.bfloat16))
                stacked = jnp.concatenate(pieces, axis=0)
                product = lax.dot_general(
                    stacked, weights_ref[i, k], (((1,), (1,)), ((), ())), preferred_element_type=f32
                )
                made = product if made is None else made + product
            trows = pl.ds(start_row, size)
            returned = (
                kept[s, i, trows]
                + in_terms[s, (PAIR - 1) * blocks + i, trows]
                + in_terms[s, (FACE - 1) * blocks + i, trows]
            )
            if with_ones:
                diag[i] = made[2 * part : 2 * part + 8] + returned[:8] + prior_ref[pl.ds(i, 1), :]
                returned = returned[8:]
            coupled = made[:part] + made[part : 2 * part] + returned
            now = ext[s][chunk][i]
            if chunk == 0:
                earlier = jnp.concatenate([now[:1], now[:-1]], axis=0)
            else:
                earlier = jnp.concatenate([ext[s][chunk - 1][i, part - 1 : part], now[:-1]], axis=0)
            if chunk == CHUNKS - 1:
                later = jnp.concatenate([now[1:], now[-1:]], axis=0)
            else:
                later = jnp.concatenate([now[1:], ext[s][chunk + 1][i, 0:1]], axis=0)
            diagonal = mask_f[i, here, :] + diag[i][:1]
            image = diagonal * now - coupled + time_tie * (2.0 * now - earlier - later)
            if s == 0:
                ext[1][chunk][i] = right[i, here, :] - image
            elif s == 1:
                ext[2][chunk][i] = image
                return (carry[0] + fold_rows(now * now), carry[1] + fold_rows(now * image))
            else:
                final[i, here, :] = image
            return carry

        zero = jnp.zeros((8, width), f32)
        return lax.fori_loop(0, blocks, row_body, (zero, zero))

    def reduce_start(index, tiles):
        for n, tile in enumerate(tiles):
            red_out[index, n] = tile
        sent = []
        for step in range(1, count):
            copy = pltpu.make_async_remote_copy(
                src_ref=red_out.at[index],
                dst_ref=red_in.at[index, step - 1],
                send_sem=red_send_sem.at[index],
                recv_sem=red_recv_sem.at[index],
                device_id={"graph": lax.rem(me + step, count)},
                device_id_type=MESH,
            )
            copy.start()

    def reduce_done(index, used):
        pltpu.make_async_copy(red_in.at[index], red_in.at[index], red_recv_sem.at[index]).wait()
        pltpu.make_async_copy(red_in.at[index], red_in.at[index], red_send_sem.at[index]).wait()
        values = []
        for n in range(used):
            tile = red_out[index, n]
            for step in range(1, count):
                tile = tile + red_in[index, step - 1, n]
            values.append(total_of(tile))
        return values

    def relay(s, chunk):
        far_terms_stage(s, chunk)
        face_relay_stage(s, chunk)
        face_terms_stage(s, chunk)
        far_relay_stage(s, chunk)

    zero = jnp.zeros((8, width), f32)
    dots = [zero, zero]
    for chunk in range(CHUNKS):
        send_stage(0, chunk)
    for i in range(blocks):
        seen = mask_ref[:, i, :].astype(f32)
        mask_f[i] = seen
        right[i] = seen * observed_ref[:, i, :]
    for s in range(APPLIED):
        for chunk in range(CHUNKS):
            relay(s, chunk)
            made = finish_stage(s, chunk)
            if s == 1:
                dots = [dots[0] + made[0], dots[1] + made[1]]
            if s + 1 < APPLIED:
                send_stage(s + 1, chunk)
        if s == 1:
            reduce_start(0, dots)
            norm_first, energy = reduce_done(0, 2)
            step_first = norm_first / energy

            def next_residual(i, carry):
                for chunk in range(CHUNKS):
                    fresh = ext[1][chunk][i] - step_first * ext[2][chunk][i]
                    right[i, pl.ds(chunk * part, part)] = fresh
                    carry = carry + fold_rows(fresh * fresh)
                return carry

            reduce_start(1, [lax.fori_loop(0, blocks, next_residual, zero)])
            (norm_second,) = reduce_done(1, 1)
            ratio = norm_second / norm_first

    def last_dot(i, carry):
        for chunk in range(CHUNKS):
            here = pl.ds(chunk * part, part)
            image = (1.0 + ratio) * ext[2][chunk][i] - step_first * final[i, here]
            direction = right[i, here] + ratio * ext[1][chunk][i]
            final[i, here] = image
            carry = carry + fold_rows(direction * image)
        return carry

    reduce_start(2, [lax.fori_loop(0, blocks, last_dot, zero)])
    (energy_second,) = reduce_done(2, 1)
    step_second = norm_second / energy_second
    for i in range(blocks):
        for chunk in range(CHUNKS):
            here = slice(chunk * part, (chunk + 1) * part)
            first = ext[1][chunk][i]
            fresh = right[i, here]
            direction = fresh + ratio * first
            solution_ref[here, i, :] = (ext[0][chunk][i] + step_first * first) + step_second * direction
            residual_ref[here, i, :] = fresh - step_second * final[i, here]
    for cond, copy in pending:
        pl.when(cond)(copy.wait_send)


def index_tables(block_cols, send_list, blocks):
    me = lax.axis_index("graph")
    core, face = me % 2, (me // 2) % 2
    listed = jnp.stack([shifted(send_list[index], "graph", offset) for index, offset in enumerate(OFFSETS)])
    role = jnp.stack(
        [
            jnp.where(core == 1, PAIR, SIDE),
            jnp.where(core == 0, PAIR, SIDE),
            jnp.where(face == 1, FACE, FAR),
            jnp.where(face == 0, FACE, FAR),
        ]
    )
    received = (role[:, None] * blocks + listed).reshape(-1)
    table = jnp.concatenate([jnp.arange(blocks, dtype=jnp.int32), received.astype(jnp.int32)])
    flat = block_cols.reshape(-1)
    places = jnp.sum(jnp.where(flat[:, None] == jnp.arange(table.shape[0])[None], table[None], 0), axis=1)
    terms = flat.shape[0]
    order = jnp.arange(terms)
    match = (places[None, :] == places[:, None]) & (order[None, :] < order[:, None])
    before = jnp.max(jnp.where(match, order[None, :], -1), axis=1)
    hits = places[None, :] == jnp.arange(5 * blocks)[:, None]
    last = jnp.max(jnp.where(hits, order[None, :], -1), axis=1)
    before = jnp.where(before < 0, terms, before)
    last = jnp.where(last < 0, terms, last)
    return places.astype(jnp.int32), before.astype(jnp.int32), last.astype(jnp.int32)


def per_device(count, observed, mask, first_guess, diag_weight, coupling, block_cols, send_rows):
    steps, blocks, width = observed.shape
    slots = coupling.shape[1]
    terms = blocks * slots
    part = steps // CHUNKS
    places, before, last = index_tables(block_cols, send_rows[0], blocks)
    f32 = jnp.float32
    vmem = pl.BlockSpec(memory_space=pltpu.VMEM)
    smem = pl.BlockSpec(memory_space=pltpu.SMEM)
    shape = jax.ShapeDtypeStruct((steps, blocks, width), f32)
    return pl.pallas_call(
        functools.partial(cg_kernel, count, blocks, slots, steps),
        out_shape=(shape, shape),
        in_specs=[smem] * 3 + [vmem] * 5,
        out_specs=(vmem, vmem),
        scratch_shapes=[pltpu.VMEM((5 * blocks, part, width), f32)] * (APPLIED * CHUNKS)
        + [
            pltpu.VMEM((blocks, steps, width), f32),
            pltpu.VMEM((blocks, steps, width), f32),
            pltpu.VMEM((blocks, steps, width), f32),
            pltpu.VMEM((terms + 1, part + 8, width), f32),
            pltpu.VMEM((APPLIED, blocks, steps + 8, width), f32),
            pltpu.VMEM((APPLIED, 4 * blocks, steps + 8, width), f32),
            pltpu.VMEM((APPLIED, 4 * blocks, steps + 8, width), f32),
            pltpu.VMEM((blocks, 8, width), f32),
            pltpu.VMEM((3, 2, 8, width), f32),
            pltpu.VMEM((3, count - 1, 2, 8, width), f32),
            pltpu.SemaphoreType.DMA((APPLIED, CHUNKS, 8)),
            pltpu.SemaphoreType.DMA((APPLIED, CHUNKS, 8)),
            pltpu.SemaphoreType.DMA((3,)),
            pltpu.SemaphoreType.DMA((3,)),
        ],
        compiler_params=pltpu.CompilerParams(
            collective_id=0, has_side_effects=True, vmem_limit_bytes=48 * 1024 * 1024
        ),
    )(places, before, last, observed, mask, first_guess, diag_weight, coupling)


def solution(mesh):
    fields = P(None, ("region", "graph"), None)
    placed = (
        fields,
        fields,
        fields,
        P(("region", "graph"), None),
        P(("region", "graph"), None, None, None),
        P(("region", "graph"), None),
        P(("region", "graph"), None, None),
    )
    return jax.shard_map(
        functools.partial(per_device, mesh.shape["graph"]),
        mesh=mesh,
        in_specs=placed,
        out_specs=(fields, fields),
        check_vma=False,
    )
```

```python
import functools

import jax
import jax.numpy as jnp
from jax import lax
from jax.experimental import pallas as pl
from jax.experimental.pallas import tpu as pltpu
from jax.sharding import PartitionSpec as P

ITERS = 2
APPLIED = ITERS + 1
OFFSETS = (1, -1, 2, -2)
time_tie = 0.5
CHUNKS = 2
UNROLL = 4
MESH = pl.DeviceIdType.MESH
OWN, PAIR, FACE, FAR, SIDE = range(5)


def split_parts(field):
    upper = field.astype(jnp.bfloat16)
    lower = (field - upper.astype(jnp.float32)).astype(jnp.bfloat16)
    return [upper, lower]


def fold_rows(values):
    total = values[0:8]
    for start in range(8, values.shape[0], 8):
        total = total + values[start : start + 8]
    return total


def total_of(tile):
    return jnp.sum(jnp.sum(tile, axis=0, keepdims=True), axis=1, keepdims=True)


def cg_kernel(
    count,
    blocks,
    slots,
    steps,
    before_ref,
    slot_last_ref,
    cols_ref,
    observed_hbm,
    mask_hbm,
    guess_hbm,
    prior_hbm,
    weights_hbm,
    lists_hbm,
    solution_ref,
    residual_ref,
    *scratch,
):
    ext = [scratch[s * CHUNKS : (s + 1) * CHUNKS] for s in range(APPLIED)]
    final, mask_f, right, sums, kept, out_terms, in_terms, diag, red_out, red_in = scratch[APPLIED * CHUNKS : -14]
    observed_ref, mask_ref, guess_ref, prior_ref, weights_ref, lists_in, lists_ref, table_ref, last_ref = scratch[-14:-5]
    send_sem, recv_sem, red_send_sem, red_recv_sem, load_sem = scratch[-5:]
    width = guess_ref.shape[2]
    places = (guess_hbm, guess_ref), (weights_hbm, weights_ref), (mask_hbm, mask_ref)
    places += (observed_hbm, observed_ref), (prior_hbm, prior_ref)
    loads = [pltpu.make_async_copy(far, near, load_sem.at[n]) for n, (far, near) in enumerate(places)]
    for load in loads:
        load.start()
    me = lax.axis_index("graph")
    core = lax.rem(me, 2)
    face = lax.rem(me // 2, 2)
    pair_id = me + 1 - 2 * core
    face_id = me + 2 - 4 * face
    far_src = me - 4 + 8 * face
    far_dst = me + 4 - 8 * face
    has_src = (far_src >= 0) & (far_src < count)
    has_dst = (far_dst >= 0) & (far_dst < count)
    same = core == face
    always = me >= 0
    part = steps // CHUNKS
    terms = blocks * slots
    f32 = jnp.float32

    barrier = pltpu.get_barrier_semaphore()
    for step in range(1, count):
        pl.semaphore_signal(barrier, inc=1, device_id={"graph": lax.rem(me + step, count)}, device_id_type=MESH)

    loads[0].wait()
    for i in range(blocks):
        for chunk in range(CHUNKS):
            ext[0][chunk][i] = guess_ref[chunk * part : (chunk + 1) * part, i, :]

    @pl.when(jnp.logical_not(has_src))
    def _():
        for held in scratch[: APPLIED * CHUNKS]:
            held[FAR * blocks : (FAR + 1) * blocks] = jnp.zeros((blocks, part, width), f32)

    @pl.when(same & jnp.logical_not(has_src))
    def _():
        for held in scratch[: APPLIED * CHUNKS]:
            held[SIDE * blocks : (SIDE + 1) * blocks] = jnp.zeros((blocks, part, width), f32)

    capacity = lists_in.shape[3]
    list_copies = []
    for index, offset in enumerate(OFFSETS):
        source, target = me - offset, me + offset
        list_copies.append(
            (
                (source >= 0) & (source < count),
                (target >= 0) & (target < count),
                pltpu.make_async_remote_copy(
                    src_ref=lists_hbm,
                    dst_ref=lists_in.at[index],
                    send_sem=load_sem.at[6 + index],
                    recv_sem=load_sem.at[10 + index],
                    device_id={"graph": target},
                    device_id_type=MESH,
                ),
            )
        )

        @pl.when((source < 0) | (source >= count))
        def _(index=index):
            lists_in[index] = jnp.zeros(lists_in.shape[1:], jnp.int32)

    sums[terms] = jnp.zeros(sums.shape[1:], f32)
    pl.semaphore_wait(barrier, count - 1)

    pending = []
    for _, wanted, copy in list_copies:
        pl.when(wanted)(copy.start)
        pending.append((wanted, copy))

    def make_tables():
        for wanted, _, copy in list_copies:
            pl.when(wanted)(copy.wait_recv)
        down = pltpu.make_async_copy(lists_in, lists_ref, load_sem.at[5])
        down.start()
        down.wait()
        roles = [
            jnp.where(core == 1, PAIR, SIDE),
            jnp.where(core == 0, PAIR, SIDE),
            jnp.where(face == 1, FACE, FAR),
            jnp.where(face == 0, FACE, FAR),
        ]
        for j in range(blocks):
            table_ref[j] = j
            last_ref[j] = slot_last_ref[j]
        for index, role in enumerate(roles):
            listed = [lists_ref[index, 0, index, e] for e in range(capacity)]
            ends = [slot_last_ref[blocks + index * capacity + e] for e in range(capacity)]
            for e in range(capacity):
                table_ref[blocks + index * capacity + e] = role * blocks + listed[e]
            for j in range(blocks):
                end = terms
                for e in range(capacity):
                    end = jnp.where(listed[e] == j, ends[e], end)
                last_ref[role * blocks + j] = end

    def field_copy(s, chunk, kind, src_role, dst_role, target):
        return pltpu.make_async_remote_copy(
            src_ref=ext[s][chunk].at[pl.ds(src_role * blocks, blocks)],
            dst_ref=ext[s][chunk].at[pl.ds(dst_role * blocks, blocks)],
            send_sem=send_sem.at[s, chunk, kind],
            recv_sem=recv_sem.at[s, chunk, kind],
            device_id={"graph": target},
            device_id_type=MESH,
        )

    def term_rows(s, chunk):
        if s == 0 and chunk == 0:
            return 0, part + 8
        return 8 + chunk * part, part

    def term_copy(s, chunk, role, target):
        start, size = term_rows(s, chunk)
        return pltpu.make_async_remote_copy(
            src_ref=out_terms.at[s, pl.ds((role - 1) * blocks, blocks), pl.ds(start, size)],
            dst_ref=in_terms.at[s, pl.ds((role - 1) * blocks, blocks), pl.ds(start, size)],
            send_sem=send_sem.at[s, chunk, 3 + role],
            recv_sem=recv_sem.at[s, chunk, 3 + role],
            device_id={"graph": target},
            device_id_type=MESH,
        )

    def start(cond, make):
        copy = make()
        pl.when(cond)(copy.start)
        pending.append((cond, copy))

    def arrived(cond, make):
        pl.when(cond)(make().wait_recv)

    def copies(s, chunk):
        field = {
            PAIR: lambda: field_copy(s, chunk, 0, OWN, PAIR, pair_id),
            FACE: lambda: field_copy(s, chunk, 1, OWN, FACE, face_id),
            FAR: lambda: field_copy(s, chunk, 2, FACE, FAR, far_dst),
            SIDE: lambda: field_copy(s, chunk, 3, FACE, SIDE, pair_id),
            "other": lambda: field_copy(s, chunk, 3, FAR, SIDE, pair_id),
        }
        term = {
            PAIR: lambda: term_copy(s, chunk, PAIR, pair_id),
            FACE: lambda: term_copy(s, chunk, FACE, face_id),
            FAR: lambda: term_copy(s, chunk, FAR, far_src),
            SIDE: lambda: term_copy(s, chunk, SIDE, pair_id),
        }
        return field, term

    def add_terms(s, chunk, role, other):
        start_row, size = term_rows(s, chunk)
        rows = pl.ds(start_row, size)

        def body(j, carry):
            at = (role - 1) * blocks + j
            out_terms[s, at, rows] = out_terms[s, at, rows] + in_terms[s, (other - 1) * blocks + j, rows]
            return carry

        lax.fori_loop(0, blocks, body, 0)

    def field_stage(s, chunk):
        field, term = copies(s, chunk)
        start(always, field[FACE])
        start(always, field[PAIR])

    def term_stage(s, chunk):
        field, term = copies(s, chunk)
        start_row, size = term_rows(s, chunk)
        with_ones = size > part
        rows = pl.ds(start_row, size)

        if with_ones:
            loads[1].wait()

        def row_body(i, carry):
            own = ext[s][chunk][i]
            pieces = split_parts(own)
            if with_ones:
                pieces.append(jnp.ones((16, own.shape[1]), jnp.bfloat16))
            stacked = jnp.concatenate(pieces, axis=0)
            for k in range(slots):
                made = jnp.dot(stacked, weights_ref[i, k], preferred_element_type=f32)
                term_now = made[:part] + made[part : 2 * part]
                if with_ones:
                    term_now = jnp.concatenate([made[2 * part : 2 * part + 8], term_now], axis=0)
                at = i * slots + k
                sums[at, :size] = term_now
            return carry

        lax.fori_loop(0, blocks, row_body, 0, unroll=UNROLL)

        def run_body(at, carry):
            sums[at, :size] = sums[at, :size] + sums[before_ref[at], :size]
            return carry

        lax.fori_loop(0, terms, run_body, 0)
        if with_ones:
            make_tables()
        for role in (SIDE, FAR, PAIR, FACE):

            def pick(j, carry, role=role):
                out_terms[s, (role - 1) * blocks + j, rows] = sums[last_ref[role * blocks + j], :size]
                return carry

            lax.fori_loop(0, blocks, pick, 0)
            if role == SIDE:
                start(jnp.logical_not(same) | has_src, term[SIDE])
            if role == FAR:
                start(same & has_src, term[FAR])
            if role == PAIR:
                start(always, term[PAIR])

        def keep(j, carry):
            kept[s, j, rows] = sums[last_ref[j], :size]
            return carry

        lax.fori_loop(0, blocks, keep, 0)

    def far_terms_stage(s, chunk):
        field, term = copies(s, chunk)
        moved = jnp.logical_not(same) & has_src
        arrived(same | has_src, term[SIDE])

        @pl.when(moved)
        def _():
            add_terms(s, chunk, FAR, SIDE)

        start(moved, term[FAR])

    def face_relay_stage(s, chunk):
        field, term = copies(s, chunk)
        arrived(always, field[FACE])
        start(has_dst, field[FAR])
        start(same, field[SIDE])

    def face_terms_stage(s, chunk):
        field, term = copies(s, chunk)

        @pl.when(same)
        def _():
            add_terms(s, chunk, FACE, SIDE)

        arrived(has_dst, term[FAR])

        @pl.when(has_dst)
        def _():
            add_terms(s, chunk, FACE, FAR)

        start(always, term[FACE])

    def far_relay_stage(s, chunk):
        field, term = copies(s, chunk)
        arrived(has_src, field[FAR])
        start(jnp.logical_not(same) & has_src, field["other"])

    def finish_stage(s, chunk):
        field, term = copies(s, chunk)
        start_row, size = term_rows(s, chunk)
        with_ones = size > part
        here = pl.ds(chunk * part, part)
        arrived(always, field[PAIR])
        arrived(jnp.logical_not(same) | has_src, field[SIDE])
        arrived(always, term[PAIR])
        arrived(always, term[FACE])

        def row_body(i, carry):
            made = None
            for k in range(slots):
                pieces = split_parts(ext[s][chunk][table_ref[cols_ref[i, k]]])
                if with_ones:
                    pieces.append(jnp.ones((16, width), jnp.bfloat16))
                stacked = jnp.concatenate(pieces, axis=0)
                product = lax.dot_general(
                    stacked, weights_ref[i, k], (((1,), (1,)), ((), ())), preferred_element_type=f32
                )
                made = product if made is None else made + product
            trows = pl.ds(start_row, size)
            returned = (
                kept[s, i, trows]
                + in_terms[s, (PAIR - 1) * blocks + i, trows]
                + in_terms[s, (FACE - 1) * blocks + i, trows]
            )
            if with_ones:
                diag[i] = made[2 * part : 2 * part + 8] + returned[:8] + prior_ref[pl.ds(i, 1), :]
                returned = returned[8:]
            coupled = made[:part] + made[part : 2 * part] + returned
            now = ext[s][chunk][i]
            if chunk == 0:
                earlier = jnp.concatenate([now[:1], now[:-1]], axis=0)
            else:
                earlier = jnp.concatenate([ext[s][chunk - 1][i, part - 1 : part], now[:-1]], axis=0)
            if chunk == CHUNKS - 1:
                later = jnp.concatenate([now[1:], now[-1:]], axis=0)
            else:
                later = jnp.concatenate([now[1:], ext[s][chunk + 1][i, 0:1]], axis=0)
            diagonal = mask_f[i, here, :] + diag[i][:1]
            image = diagonal * now - coupled + time_tie * (2.0 * now - earlier - later)
            if s == 0:
                ext[1][chunk][i] = right[i, here, :] - image
            elif s == 1:
                ext[2][chunk][i] = image
                return (carry[0] + fold_rows(now * now), carry[1] + fold_rows(now * image))
            else:
                final[i, here, :] = image
            return carry

        zero = jnp.zeros((8, width), f32)
        return lax.fori_loop(0, blocks, row_body, (zero, zero), unroll=UNROLL)

    def reduce_start(index, tiles):
        for n, tile in enumerate(tiles):
            red_out[index, n] = tile
        sent = []
        for step in range(1, count):
            copy = pltpu.make_async_remote_copy(
                src_ref=red_out.at[index],
                dst_ref=red_in.at[index, step - 1],
                send_sem=red_send_sem.at[index],
                recv_sem=red_recv_sem.at[index],
                device_id={"graph": lax.rem(me + step, count)},
                device_id_type=MESH,
            )
            copy.start()

    def reduce_done(index, used):
        pltpu.make_async_copy(red_in.at[index], red_in.at[index], red_recv_sem.at[index]).wait()
        pltpu.make_async_copy(red_in.at[index], red_in.at[index], red_send_sem.at[index]).wait()
        values = []
        for n in range(used):
            tile = red_out[index, n]
            for step in range(1, count):
                tile = tile + red_in[index, step - 1, n]
            values.append(total_of(tile))
        return values

    def relay(s, chunk):
        far_terms_stage(s, chunk)
        face_relay_stage(s, chunk)
        face_terms_stage(s, chunk)
        far_relay_stage(s, chunk)

    zero = jnp.zeros((8, width), f32)
    dots = [zero, zero]
    for chunk in range(CHUNKS):
        field_stage(0, chunk)
    for chunk in range(CHUNKS):
        term_stage(0, chunk)
    for load in loads[2:]:
        load.wait()
    for i in range(blocks):
        seen = mask_ref[:, i, :].astype(f32)
        mask_f[i] = seen
        right[i] = seen * observed_ref[:, i, :]
    for s in range(APPLIED):
        for stage in (far_terms_stage, face_relay_stage, face_terms_stage, far_relay_stage):
            for chunk in range(CHUNKS):
                stage(s, chunk)
        for chunk in range(CHUNKS):
            made = finish_stage(s, chunk)
            if s == 1:
                dots = [dots[0] + made[0], dots[1] + made[1]]
            if s + 1 < APPLIED:
                field_stage(s + 1, chunk)
        if s + 1 < APPLIED:
            for chunk in range(CHUNKS):
                term_stage(s + 1, chunk)
        if s == 1:
            reduce_start(0, dots)
            norm_first, energy = reduce_done(0, 2)
            step_first = norm_first / energy

            def next_residual(i, carry):
                for chunk in range(CHUNKS):
                    fresh = ext[1][chunk][i] - step_first * ext[2][chunk][i]
                    right[i, pl.ds(chunk * part, part)] = fresh
                    carry = carry + fold_rows(fresh * fresh)
                return carry

            reduce_start(1, [lax.fori_loop(0, blocks, next_residual, zero)])
            (norm_second,) = reduce_done(1, 1)
            ratio = norm_second / norm_first

    def last_dot(i, carry):
        for chunk in range(CHUNKS):
            here = pl.ds(chunk * part, part)
            image = (1.0 + ratio) * ext[2][chunk][i] - step_first * final[i, here]
            direction = right[i, here] + ratio * ext[1][chunk][i]
            final[i, here] = image
            carry = carry + fold_rows(direction * image)
        return carry

    reduce_start(2, [lax.fori_loop(0, blocks, last_dot, zero)])
    (energy_second,) = reduce_done(2, 1)
    step_second = norm_second / energy_second
    for i in range(blocks):
        for chunk in range(CHUNKS):
            here = slice(chunk * part, (chunk + 1) * part)
            first = ext[1][chunk][i]
            fresh = right[i, here]
            direction = fresh + ratio * first
            solution_ref[here, i, :] = (ext[0][chunk][i] + step_first * first) + step_second * direction
            residual_ref[here, i, :] = fresh - step_second * final[i, here]
    for cond, copy in pending:
        pl.when(cond)(copy.wait_send)


def index_tables(block_cols, ext_count):
    flat = block_cols.reshape(-1)
    terms = flat.shape[0]
    order = jnp.arange(terms, dtype=jnp.int32)
    match = (flat[None, :] == flat[:, None]) & (order[None, :] < order[:, None])
    before = jnp.max(jnp.where(match, order[None, :], -1), axis=1)
    hits = flat[None, :] == jnp.arange(ext_count, dtype=jnp.int32)[:, None]
    last = jnp.max(jnp.where(hits, order[None, :], -1), axis=1)
    return jnp.where(before < 0, terms, before), jnp.where(last < 0, terms, last)


def per_device(count, observed, mask, first_guess, diag_weight, coupling, block_cols, send_rows):
    steps, blocks, width = observed.shape
    slots = coupling.shape[1]
    terms = blocks * slots
    part = steps // CHUNKS
    ext_count = blocks + 4 * send_rows.shape[2]
    before, last = index_tables(block_cols, ext_count)
    f32 = jnp.float32
    vmem = pl.BlockSpec(memory_space=pltpu.VMEM)
    smem = pl.BlockSpec(memory_space=pltpu.SMEM)
    shape = jax.ShapeDtypeStruct((steps, blocks, width), f32)
    return pl.pallas_call(
        functools.partial(cg_kernel, count, blocks, slots, steps),
        out_shape=(shape, shape),
        in_specs=[smem] * 3 + [pl.BlockSpec(memory_space=pl.ANY)] * 6,
        out_specs=(vmem, vmem),
        scratch_shapes=[pltpu.VMEM((5 * blocks, part, width), f32)] * (APPLIED * CHUNKS)
        + [
            pltpu.VMEM((blocks, steps, width), f32),
            pltpu.VMEM((blocks, steps, width), f32),
            pltpu.VMEM((blocks, steps, width), f32),
            pltpu.VMEM((terms + 1, part + 8, width), f32),
            pltpu.VMEM((APPLIED, blocks, steps + 8, width), f32),
            pltpu.VMEM((APPLIED, 4 * blocks, steps + 8, width), f32),
            pltpu.VMEM((APPLIED, 4 * blocks, steps + 8, width), f32),
            pltpu.VMEM((blocks, 8, width), f32),
            pltpu.VMEM((3, 2, 8, width), f32),
            pltpu.VMEM((3, count - 1, 2, 8, width), f32),
            pltpu.VMEM(observed.shape, f32),
            pltpu.VMEM(mask.shape, mask.dtype),
            pltpu.VMEM(first_guess.shape, f32),
            pltpu.VMEM(diag_weight.shape, f32),
            pltpu.VMEM(coupling.shape, coupling.dtype),
            pltpu.VMEM((4,) + send_rows.shape, jnp.int32),
            pltpu.SMEM((4,) + send_rows.shape, jnp.int32),
            pltpu.SMEM((ext_count,), jnp.int32),
            pltpu.SMEM((5 * blocks,), jnp.int32),
            pltpu.SemaphoreType.DMA((APPLIED, CHUNKS, 8)),
            pltpu.SemaphoreType.DMA((APPLIED, CHUNKS, 8)),
            pltpu.SemaphoreType.DMA((3,)),
            pltpu.SemaphoreType.DMA((3,)),
            pltpu.SemaphoreType.DMA((14,)),
        ],
        compiler_params=pltpu.CompilerParams(
            collective_id=0, has_side_effects=True, vmem_limit_bytes=48 * 1024 * 1024
        ),
    )(before, last, block_cols, observed, mask, first_guess, diag_weight, coupling, send_rows)


def solution(mesh):
    fields = P(None, ("region", "graph"), None)
    placed = (
        fields,
        fields,
        fields,
        P(("region", "graph"), None),
        P(("region", "graph"), None, None, None),
        P(("region", "graph"), None),
        P(("region", "graph"), None, None),
    )
    return jax.shard_map(
        functools.partial(per_device, mesh.shape["graph"]),
        mesh=mesh,
        in_specs=placed,
        out_specs=(fields, fields),
        check_vma=False,
    )
```

```python
import functools

import jax
import jax.numpy as jnp
from jax import lax
from jax.experimental import pallas as pl
from jax.experimental.pallas import tpu as pltpu
from jax.sharding import PartitionSpec as P

ITERS = 2
APPLIED = ITERS + 1
OFFSETS = (1, -1, 2, -2)
time_tie = 0.5
CHUNKS = 2
UNROLL = 4
LIMIT = 60
MESH = pl.DeviceIdType.MESH
OWN, PAIR, FACE, FAR, SIDE = range(5)


def split_parts(field):
    upper = field.astype(jnp.bfloat16)
    lower = (field - upper.astype(jnp.float32)).astype(jnp.bfloat16)
    return [upper, lower]


def fold_rows(values):
    total = values[0:8]
    for start in range(8, values.shape[0], 8):
        total = total + values[start : start + 8]
    return total


def total_of(tile):
    return jnp.sum(jnp.sum(tile, axis=0, keepdims=True), axis=1, keepdims=True)


def cg_kernel(
    count,
    blocks,
    slots,
    steps,
    before_ref,
    slot_last_ref,
    cols_ref,
    observed_hbm,
    mask_hbm,
    guess_hbm,
    prior_hbm,
    weights_hbm,
    lists_hbm,
    solution_ref,
    residual_ref,
    *scratch,
):
    ext = [scratch[s * CHUNKS : (s + 1) * CHUNKS] for s in range(APPLIED)]
    final, mask_f, right, sums, kept, out_terms, in_terms, diag, red_out, red_in = scratch[APPLIED * CHUNKS : -14]
    observed_ref, mask_ref, guess_ref, prior_ref, weights_ref, lists_in, lists_ref, table_ref, last_ref = scratch[-14:-5]
    send_sem, recv_sem, red_send_sem, red_recv_sem, load_sem = scratch[-5:]
    width = guess_ref.shape[2]
    places = (guess_hbm, guess_ref), (weights_hbm, weights_ref), (mask_hbm, mask_ref)
    places += (observed_hbm, observed_ref), (prior_hbm, prior_ref)
    loads = [pltpu.make_async_copy(far, near, load_sem.at[n]) for n, (far, near) in enumerate(places)]
    for load in loads:
        load.start()
    me = lax.axis_index("graph")
    core = lax.rem(me, 2)
    face = lax.rem(me // 2, 2)
    pair_id = me + 1 - 2 * core
    face_id = me + 2 - 4 * face
    far_src = me - 4 + 8 * face
    far_dst = me + 4 - 8 * face
    has_src = (far_src >= 0) & (far_src < count)
    has_dst = (far_dst >= 0) & (far_dst < count)
    same = core == face
    always = me >= 0
    part = steps // CHUNKS
    terms = blocks * slots
    f32 = jnp.float32

    barrier = pltpu.get_barrier_semaphore()
    for step in range(1, count):
        pl.semaphore_signal(barrier, inc=1, device_id={"graph": lax.rem(me + step, count)}, device_id_type=MESH)

    loads[0].wait()
    for i in range(blocks):
        for chunk in range(CHUNKS):
            ext[0][chunk][i] = guess_ref[chunk * part : (chunk + 1) * part, i, :]

    @pl.when(jnp.logical_not(has_src))
    def _():
        for held in scratch[: APPLIED * CHUNKS]:
            held[FAR * blocks : (FAR + 1) * blocks] = jnp.zeros((blocks, part, width), f32)

    @pl.when(same & jnp.logical_not(has_src))
    def _():
        for held in scratch[: APPLIED * CHUNKS]:
            held[SIDE * blocks : (SIDE + 1) * blocks] = jnp.zeros((blocks, part, width), f32)

    capacity = lists_in.shape[3]
    list_copies = []
    for index, offset in enumerate(OFFSETS):
        source, target = me - offset, me + offset
        list_copies.append(
            (
                (source >= 0) & (source < count),
                (target >= 0) & (target < count),
                pltpu.make_async_remote_copy(
                    src_ref=lists_hbm,
                    dst_ref=lists_in.at[index],
                    send_sem=load_sem.at[6 + index],
                    recv_sem=load_sem.at[10 + index],
                    device_id={"graph": target},
                    device_id_type=MESH,
                ),
            )
        )

        @pl.when((source < 0) | (source >= count))
        def _(index=index):
            lists_in[index] = jnp.zeros(lists_in.shape[1:], jnp.int32)

    sums[terms] = jnp.zeros(sums.shape[1:], f32)
    pl.semaphore_wait(barrier, count - 1)

    pending = []
    for _, wanted, copy in list_copies:
        pl.when(wanted)(copy.start)
        pending.append((wanted, copy))

    def make_tables():
        for wanted, _, copy in list_copies:
            pl.when(wanted)(copy.wait_recv)
        down = pltpu.make_async_copy(lists_in, lists_ref, load_sem.at[5])
        down.start()
        down.wait()
        roles = [
            jnp.where(core == 1, PAIR, SIDE),
            jnp.where(core == 0, PAIR, SIDE),
            jnp.where(face == 1, FACE, FAR),
            jnp.where(face == 0, FACE, FAR),
        ]
        for j in range(blocks):
            table_ref[j] = j
            last_ref[j] = slot_last_ref[j]
        for index, role in enumerate(roles):
            listed = [lists_ref[index, 0, index, e] for e in range(capacity)]
            ends = [slot_last_ref[blocks + index * capacity + e] for e in range(capacity)]
            for e in range(capacity):
                table_ref[blocks + index * capacity + e] = role * blocks + listed[e]
            for j in range(blocks):
                end = terms
                for e in range(capacity):
                    end = jnp.where(listed[e] == j, ends[e], end)
                last_ref[role * blocks + j] = end

    def field_copy(s, chunk, kind, src_role, dst_role, target):
        return pltpu.make_async_remote_copy(
            src_ref=ext[s][chunk].at[pl.ds(src_role * blocks, blocks)],
            dst_ref=ext[s][chunk].at[pl.ds(dst_role * blocks, blocks)],
            send_sem=send_sem.at[s, chunk, kind],
            recv_sem=recv_sem.at[s, chunk, kind],
            device_id={"graph": target},
            device_id_type=MESH,
        )

    def term_rows(s, chunk):
        if s == 0 and chunk == 0:
            return 0, part + 8
        return 8 + chunk * part, part

    def term_copy(s, chunk, role, target):
        start, size = term_rows(s, chunk)
        return pltpu.make_async_remote_copy(
            src_ref=out_terms.at[s, pl.ds((role - 1) * blocks, blocks), pl.ds(start, size)],
            dst_ref=in_terms.at[s, pl.ds((role - 1) * blocks, blocks), pl.ds(start, size)],
            send_sem=send_sem.at[s, chunk, 3 + role],
            recv_sem=recv_sem.at[s, chunk, 3 + role],
            device_id={"graph": target},
            device_id_type=MESH,
        )

    def start(cond, make):
        copy = make()
        pl.when(cond)(copy.start)
        pending.append((cond, copy))

    def arrived(cond, make):
        pl.when(cond)(make().wait_recv)

    def copies(s, chunk):
        field = {
            PAIR: lambda: field_copy(s, chunk, 0, OWN, PAIR, pair_id),
            FACE: lambda: field_copy(s, chunk, 1, OWN, FACE, face_id),
            FAR: lambda: field_copy(s, chunk, 2, FACE, FAR, far_dst),
            SIDE: lambda: field_copy(s, chunk, 3, FACE, SIDE, pair_id),
            "other": lambda: field_copy(s, chunk, 3, FAR, SIDE, pair_id),
        }
        term = {
            PAIR: lambda: term_copy(s, chunk, PAIR, pair_id),
            FACE: lambda: term_copy(s, chunk, FACE, face_id),
            FAR: lambda: term_copy(s, chunk, FAR, far_src),
            SIDE: lambda: term_copy(s, chunk, SIDE, pair_id),
        }
        return field, term

    def add_terms(s, chunk, role, other):
        start_row, size = term_rows(s, chunk)
        rows = pl.ds(start_row, size)

        def body(j, carry):
            at = (role - 1) * blocks + j
            out_terms[s, at, rows] = out_terms[s, at, rows] + in_terms[s, (other - 1) * blocks + j, rows]
            return carry

        lax.fori_loop(0, blocks, body, 0)

    def field_stage(s, chunk):
        field, term = copies(s, chunk)
        start(always, field[FACE])
        start(always, field[PAIR])

    def term_stage(s, chunk):
        field, term = copies(s, chunk)
        start_row, size = term_rows(s, chunk)
        with_ones = size > part
        rows = pl.ds(start_row, size)

        if with_ones:
            loads[1].wait()

        def row_body(i, carry):
            own = ext[s][chunk][i]
            pieces = split_parts(own)
            if with_ones:
                pieces.append(jnp.ones((16, own.shape[1]), jnp.bfloat16))
            stacked = jnp.concatenate(pieces, axis=0)
            for k in range(slots):
                made = jnp.dot(stacked, weights_ref[i, k], preferred_element_type=f32)
                term_now = made[:part] + made[part : 2 * part]
                if with_ones:
                    term_now = jnp.concatenate([made[2 * part : 2 * part + 8], term_now], axis=0)
                at = i * slots + k
                sums[at, :size] = term_now
            return carry

        lax.fori_loop(0, blocks, row_body, 0, unroll=UNROLL)

        def run_body(at, carry):
            sums[at, :size] = sums[at, :size] + sums[before_ref[at], :size]
            return carry

        lax.fori_loop(0, terms, run_body, 0)
        if with_ones:
            make_tables()
        for role in (SIDE, FAR, PAIR, FACE):

            def pick(j, carry, role=role):
                out_terms[s, (role - 1) * blocks + j, rows] = sums[last_ref[role * blocks + j], :size]
                return carry

            lax.fori_loop(0, blocks, pick, 0)
            if role == SIDE:
                start(jnp.logical_not(same) | has_src, term[SIDE])
            if role == FAR:
                start(same & has_src, term[FAR])
            if role == PAIR:
                start(always, term[PAIR])

        def keep(j, carry):
            kept[s, j, rows] = sums[last_ref[j], :size]
            return carry

        lax.fori_loop(0, blocks, keep, 0)

    def far_terms_stage(s, chunk):
        field, term = copies(s, chunk)
        moved = jnp.logical_not(same) & has_src
        arrived(same | has_src, term[SIDE])

        @pl.when(moved)
        def _():
            add_terms(s, chunk, FAR, SIDE)

        start(moved, term[FAR])

    def face_relay_stage(s, chunk):
        field, term = copies(s, chunk)
        arrived(always, field[FACE])
        start(has_dst, field[FAR])
        start(same, field[SIDE])

    def face_terms_stage(s, chunk):
        field, term = copies(s, chunk)

        @pl.when(same)
        def _():
            add_terms(s, chunk, FACE, SIDE)

        arrived(has_dst, term[FAR])

        @pl.when(has_dst)
        def _():
            add_terms(s, chunk, FACE, FAR)

        start(always, term[FACE])

    def far_relay_stage(s, chunk):
        field, term = copies(s, chunk)
        arrived(has_src, field[FAR])
        start(jnp.logical_not(same) & has_src, field["other"])

    def finish_stage(s, chunk):
        field, term = copies(s, chunk)
        start_row, size = term_rows(s, chunk)
        with_ones = size > part
        here = pl.ds(chunk * part, part)
        arrived(always, field[PAIR])
        arrived(jnp.logical_not(same) | has_src, field[SIDE])
        arrived(always, term[PAIR])
        arrived(always, term[FACE])

        def row_body(i, carry):
            made = None
            for k in range(slots):
                pieces = split_parts(ext[s][chunk][table_ref[cols_ref[i, k]]])
                if with_ones:
                    pieces.append(jnp.ones((16, width), jnp.bfloat16))
                stacked = jnp.concatenate(pieces, axis=0)
                product = lax.dot_general(
                    stacked, weights_ref[i, k], (((1,), (1,)), ((), ())), preferred_element_type=f32
                )
                made = product if made is None else made + product
            trows = pl.ds(start_row, size)
            returned = (
                kept[s, i, trows]
                + in_terms[s, (PAIR - 1) * blocks + i, trows]
                + in_terms[s, (FACE - 1) * blocks + i, trows]
            )
            if with_ones:
                diag[i] = made[2 * part : 2 * part + 8] + returned[:8] + prior_ref[pl.ds(i, 1), :]
                returned = returned[8:]
            coupled = made[:part] + made[part : 2 * part] + returned
            now = ext[s][chunk][i]
            if chunk == 0:
                earlier = jnp.concatenate([now[:1], now[:-1]], axis=0)
            else:
                earlier = jnp.concatenate([ext[s][chunk - 1][i, part - 1 : part], now[:-1]], axis=0)
            if chunk == CHUNKS - 1:
                later = jnp.concatenate([now[1:], now[-1:]], axis=0)
            else:
                later = jnp.concatenate([now[1:], ext[s][chunk + 1][i, 0:1]], axis=0)
            diagonal = mask_f[i, here, :] + diag[i][:1]
            image = diagonal * now - coupled + time_tie * (2.0 * now - earlier - later)
            if s == 0:
                ext[1][chunk][i] = right[i, here, :] - image
            elif s == 1:
                ext[2][chunk][i] = image
                return (carry[0] + fold_rows(now * now), carry[1] + fold_rows(now * image))
            else:
                final[i, here, :] = image
            return carry

        zero = jnp.zeros((8, width), f32)
        return lax.fori_loop(0, blocks, row_body, (zero, zero), unroll=UNROLL)

    def reduce_start(index, tiles):
        for n, tile in enumerate(tiles):
            red_out[index, n] = tile
        sent = []
        for step in range(1, count):
            copy = pltpu.make_async_remote_copy(
                src_ref=red_out.at[index],
                dst_ref=red_in.at[index, step - 1],
                send_sem=red_send_sem.at[index],
                recv_sem=red_recv_sem.at[index],
                device_id={"graph": lax.rem(me + step, count)},
                device_id_type=MESH,
            )
            copy.start()

    def reduce_done(index, used):
        pltpu.make_async_copy(red_in.at[index], red_in.at[index], red_recv_sem.at[index]).wait()
        pltpu.make_async_copy(red_in.at[index], red_in.at[index], red_send_sem.at[index]).wait()
        values = []
        for n in range(used):
            tile = red_out[index, n]
            for step in range(1, count):
                tile = tile + red_in[index, step - 1, n]
            values.append(total_of(tile))
        return values

    def relay(s, chunk):
        far_terms_stage(s, chunk)
        face_relay_stage(s, chunk)
        face_terms_stage(s, chunk)
        far_relay_stage(s, chunk)

    zero = jnp.zeros((8, width), f32)
    for chunk in range(CHUNKS):
        field_stage(0, chunk)
    for chunk in range(CHUNKS):
        term_stage(0, chunk)
        far_terms_stage(0, chunk)
    for load in loads[2:]:
        load.wait()
    for i in range(blocks):
        seen = mask_ref[:, i, :].astype(f32)
        mask_f[i] = seen
        right[i] = seen * observed_ref[:, i, :]
    for s in range(APPLIED):
        for chunk in range(CHUNKS):
            face_relay_stage(s, chunk)
        if s == 2:
            norm_first, energy = reduce_done(0, 2)
            step_first = norm_first / energy

            def next_residual(i, carry):
                for chunk in range(CHUNKS):
                    fresh = ext[1][chunk][i] - step_first * ext[2][chunk][i]
                    right[i, pl.ds(chunk * part, part)] = fresh
                    carry = carry + fold_rows(fresh * fresh)
                return carry

            reduce_start(1, [lax.fori_loop(0, blocks, next_residual, zero)])
        for chunk in range(CHUNKS):
            face_terms_stage(s, chunk)
            far_relay_stage(s, chunk)
        dots = [zero, zero]
        for chunk in range(CHUNKS):
            made = finish_stage(s, chunk)
            dots = [dots[0] + made[0], dots[1] + made[1]]
            if s + 1 < APPLIED:
                field_stage(s + 1, chunk)
                if s == 1 and chunk == CHUNKS - 1:
                    reduce_start(0, dots)
                term_stage(s + 1, chunk)
                far_terms_stage(s + 1, chunk)
    (norm_second,) = reduce_done(1, 1)
    ratio = norm_second / norm_first

    def last_dot(i, carry):
        for chunk in range(CHUNKS):
            here = pl.ds(chunk * part, part)
            image = (1.0 + ratio) * ext[2][chunk][i] - step_first * final[i, here]
            direction = right[i, here] + ratio * ext[1][chunk][i]
            final[i, here] = image
            carry = carry + fold_rows(direction * image)
        return carry

    reduce_start(2, [lax.fori_loop(0, blocks, last_dot, zero)])
    (energy_second,) = reduce_done(2, 1)
    step_second = norm_second / energy_second
    for i in range(blocks):
        for chunk in range(CHUNKS):
            here = slice(chunk * part, (chunk + 1) * part)
            first = ext[1][chunk][i]
            fresh = right[i, here]
            direction = fresh + ratio * first
            solution_ref[here, i, :] = (ext[0][chunk][i] + step_first * first) + step_second * direction
            residual_ref[here, i, :] = fresh - step_second * final[i, here]
    for cond, copy in pending:
        pl.when(cond)(copy.wait_send)


def index_tables(block_cols, ext_count):
    flat = block_cols.reshape(-1)
    terms = flat.shape[0]
    order = jnp.arange(terms, dtype=jnp.int32)
    match = (flat[None, :] == flat[:, None]) & (order[None, :] < order[:, None])
    before = jnp.max(jnp.where(match, order[None, :], -1), axis=1)
    hits = flat[None, :] == jnp.arange(ext_count, dtype=jnp.int32)[:, None]
    last = jnp.max(jnp.where(hits, order[None, :], -1), axis=1)
    return jnp.where(before < 0, terms, before), jnp.where(last < 0, terms, last)


def per_device(count, observed, mask, first_guess, diag_weight, coupling, block_cols, send_rows):
    steps, blocks, width = observed.shape
    slots = coupling.shape[1]
    terms = blocks * slots
    part = steps // CHUNKS
    ext_count = blocks + 4 * send_rows.shape[2]
    before, last = index_tables(block_cols, ext_count)
    f32 = jnp.float32
    vmem = pl.BlockSpec(memory_space=pltpu.VMEM)
    smem = pl.BlockSpec(memory_space=pltpu.SMEM)
    shape = jax.ShapeDtypeStruct((steps, blocks, width), f32)
    return pl.pallas_call(
        functools.partial(cg_kernel, count, blocks, slots, steps),
        out_shape=(shape, shape),
        in_specs=[smem] * 3 + [pl.BlockSpec(memory_space=pl.ANY)] * 6,
        out_specs=(vmem, vmem),
        scratch_shapes=[pltpu.VMEM((5 * blocks, part, width), f32)] * (APPLIED * CHUNKS)
        + [
            pltpu.VMEM((blocks, steps, width), f32),
            pltpu.VMEM((blocks, steps, width), f32),
            pltpu.VMEM((blocks, steps, width), f32),
            pltpu.VMEM((terms + 1, part + 8, width), f32),
            pltpu.VMEM((APPLIED, blocks, steps + 8, width), f32),
            pltpu.VMEM((APPLIED, 4 * blocks, steps + 8, width), f32),
            pltpu.VMEM((APPLIED, 4 * blocks, steps + 8, width), f32),
            pltpu.VMEM((blocks, 8, width), f32),
            pltpu.VMEM((3, 2, 8, width), f32),
            pltpu.VMEM((3, count - 1, 2, 8, width), f32),
            pltpu.VMEM(observed.shape, f32),
            pltpu.VMEM(mask.shape, mask.dtype),
            pltpu.VMEM(first_guess.shape, f32),
            pltpu.VMEM(diag_weight.shape, f32),
            pltpu.VMEM(coupling.shape, coupling.dtype),
            pltpu.VMEM((4,) + send_rows.shape, jnp.int32),
            pltpu.SMEM((4,) + send_rows.shape, jnp.int32),
            pltpu.SMEM((ext_count,), jnp.int32),
            pltpu.SMEM((5 * blocks,), jnp.int32),
            pltpu.SemaphoreType.DMA((APPLIED, CHUNKS, 8)),
            pltpu.SemaphoreType.DMA((APPLIED, CHUNKS, 8)),
            pltpu.SemaphoreType.DMA((3,)),
            pltpu.SemaphoreType.DMA((3,)),
            pltpu.SemaphoreType.DMA((14,)),
        ],
        compiler_params=pltpu.CompilerParams(
            collective_id=0, has_side_effects=True, vmem_limit_bytes=LIMIT * 1024 * 1024
        ),
    )(before, last, block_cols, observed, mask, first_guess, diag_weight, coupling, send_rows)


def solution(mesh):
    fields = P(None, ("region", "graph"), None)
    placed = (
        fields,
        fields,
        fields,
        P(("region", "graph"), None),
        P(("region", "graph"), None, None, None),
        P(("region", "graph"), None),
        P(("region", "graph"), None, None),
    )
    return jax.shard_map(
        functools.partial(per_device, mesh.shape["graph"]),
        mesh=mesh,
        in_specs=placed,
        out_specs=(fields, fields),
        check_vma=False,
    )
```

```python
import functools

import jax
import jax.numpy as jnp
from jax import lax
from jax.experimental import pallas as pl
from jax.experimental.pallas import tpu as pltpu
from jax.sharding import PartitionSpec as P

ITERS = 2
APPLIED = ITERS + 1
OFFSETS = (1, -1, 2, -2)
time_tie = 0.5
CHUNKS = 2
UNROLL = 4
LIMIT = 60
MESH = pl.DeviceIdType.MESH
OWN, PAIR, FACE, FAR, SIDE = range(5)


def split_parts(field):
    upper = field.astype(jnp.bfloat16)
    lower = (field - upper.astype(jnp.float32)).astype(jnp.bfloat16)
    return [upper, lower]


def fold_rows(values):
    total = values[0:8]
    for start in range(8, values.shape[0], 8):
        total = total + values[start : start + 8]
    return total


def total_of(tile):
    return jnp.sum(jnp.sum(tile, axis=0, keepdims=True), axis=1, keepdims=True)


def cg_kernel(
    count,
    blocks,
    slots,
    steps,
    before_ref,
    slot_last_ref,
    cols_ref,
    observed_hbm,
    mask_hbm,
    guess_hbm,
    prior_hbm,
    weights_hbm,
    lists_hbm,
    solution_ref,
    residual_ref,
    *scratch,
):
    ext = [scratch[s * CHUNKS : (s + 1) * CHUNKS] for s in range(APPLIED)]
    final, mask_f, right, forward, sums, kept, out_terms, in_terms, diag, red_out, red_in = scratch[APPLIED * CHUNKS : -14]
    observed_ref, mask_ref, guess_ref, prior_ref, weights_ref, lists_in, lists_ref, table_ref, last_ref = scratch[-14:-5]
    send_sem, recv_sem, red_send_sem, red_recv_sem, load_sem = scratch[-5:]
    width = guess_ref.shape[2]
    places = (guess_hbm, guess_ref), (weights_hbm, weights_ref), (mask_hbm, mask_ref)
    places += (observed_hbm, observed_ref), (prior_hbm, prior_ref)
    loads = [pltpu.make_async_copy(far, near, load_sem.at[n]) for n, (far, near) in enumerate(places)]
    for load in loads:
        load.start()
    me = lax.axis_index("graph")
    core = lax.rem(me, 2)
    face = lax.rem(me // 2, 2)
    pair_id = me + 1 - 2 * core
    face_id = me + 2 - 4 * face
    far_src = me - 4 + 8 * face
    far_dst = me + 4 - 8 * face
    has_src = (far_src >= 0) & (far_src < count)
    has_dst = (far_dst >= 0) & (far_dst < count)
    same = core == face
    always = me >= 0
    part = steps // CHUNKS
    terms = blocks * slots
    f32 = jnp.float32

    barrier = pltpu.get_barrier_semaphore()
    for step in range(1, count):
        pl.semaphore_signal(barrier, inc=1, device_id={"graph": lax.rem(me + step, count)}, device_id_type=MESH)

    loads[0].wait()
    for i in range(blocks):
        for chunk in range(CHUNKS):
            ext[0][chunk][i] = guess_ref[chunk * part : (chunk + 1) * part, i, :]

    @pl.when(jnp.logical_not(has_src))
    def _():
        for held in scratch[: APPLIED * CHUNKS]:
            held[FAR * blocks : (FAR + 1) * blocks] = jnp.zeros((blocks, part, width), f32)

    @pl.when(same & jnp.logical_not(has_src))
    def _():
        for held in scratch[: APPLIED * CHUNKS]:
            held[SIDE * blocks : (SIDE + 1) * blocks] = jnp.zeros((blocks, part, width), f32)

    capacity = lists_in.shape[3]
    list_copies = []
    for index, offset in enumerate(OFFSETS):
        source, target = me - offset, me + offset
        list_copies.append(
            (
                (source >= 0) & (source < count),
                (target >= 0) & (target < count),
                pltpu.make_async_remote_copy(
                    src_ref=lists_hbm,
                    dst_ref=lists_in.at[index],
                    send_sem=load_sem.at[6 + index],
                    recv_sem=load_sem.at[10 + index],
                    device_id={"graph": target},
                    device_id_type=MESH,
                ),
            )
        )

        @pl.when((source < 0) | (source >= count))
        def _(index=index):
            lists_in[index] = jnp.zeros(lists_in.shape[1:], jnp.int32)

    sums[terms] = jnp.zeros(sums.shape[1:], f32)
    pl.semaphore_wait(barrier, count - 1)

    pending = []
    for _, wanted, copy in list_copies:
        pl.when(wanted)(copy.start)
        pending.append((wanted, copy))

    def make_tables():
        for wanted, _, copy in list_copies:
            pl.when(wanted)(copy.wait_recv)
        down = pltpu.make_async_copy(lists_in, lists_ref, load_sem.at[5])
        down.start()
        down.wait()
        roles = [
            jnp.where(core == 1, PAIR, SIDE),
            jnp.where(core == 0, PAIR, SIDE),
            jnp.where(face == 1, FACE, FAR),
            jnp.where(face == 0, FACE, FAR),
        ]
        for j in range(blocks):
            table_ref[j] = j
            last_ref[j] = slot_last_ref[j]
        for index, role in enumerate(roles):
            listed = [lists_ref[index, 0, index, e] for e in range(capacity)]
            ends = [slot_last_ref[blocks + index * capacity + e] for e in range(capacity)]
            for e in range(capacity):
                table_ref[blocks + index * capacity + e] = role * blocks + listed[e]
            for j in range(blocks):
                end = terms
                for e in range(capacity):
                    end = jnp.where(listed[e] == j, ends[e], end)
                last_ref[role * blocks + j] = end

    def field_copy(s, chunk, kind, src_role, dst_role, target):
        return pltpu.make_async_remote_copy(
            src_ref=ext[s][chunk].at[pl.ds(src_role * blocks, blocks)],
            dst_ref=ext[s][chunk].at[pl.ds(dst_role * blocks, blocks)],
            send_sem=send_sem.at[s, chunk, kind],
            recv_sem=recv_sem.at[s, chunk, kind],
            device_id={"graph": target},
            device_id_type=MESH,
        )

    def term_rows(s, chunk):
        if s == 0 and chunk == 0:
            return 0, part + 8
        return 8 + chunk * part, part

    def term_copy(s, chunk, role, target):
        start, size = term_rows(s, chunk)
        return pltpu.make_async_remote_copy(
            src_ref=out_terms.at[s, pl.ds((role - 1) * blocks, blocks), pl.ds(start, size)],
            dst_ref=in_terms.at[s, pl.ds((role - 1) * blocks, blocks), pl.ds(start, size)],
            send_sem=send_sem.at[s, chunk, 3 + role],
            recv_sem=recv_sem.at[s, chunk, 3 + role],
            device_id={"graph": target},
            device_id_type=MESH,
        )

    def start(cond, make):
        copy = make()
        pl.when(cond)(copy.start)
        pending.append((cond, copy))

    def arrived(cond, make):
        pl.when(cond)(make().wait_recv)

    def copies(s, chunk):
        field = {
            PAIR: lambda: field_copy(s, chunk, 0, OWN, PAIR, pair_id),
            FACE: lambda: field_copy(s, chunk, 1, OWN, FACE, face_id),
            FAR: lambda: field_copy(s, chunk, 2, FACE, FAR, far_dst),
            SIDE: lambda: field_copy(s, chunk, 3, FACE, SIDE, pair_id),
            "other": lambda: field_copy(s, chunk, 3, FAR, SIDE, pair_id),
        }
        term = {
            PAIR: lambda: term_copy(s, chunk, PAIR, pair_id),
            FACE: lambda: term_copy(s, chunk, FACE, face_id),
            FAR: lambda: term_copy(s, chunk, FAR, far_src),
            SIDE: lambda: term_copy(s, chunk, SIDE, pair_id),
        }
        return field, term

    def add_terms(s, chunk, role, other):
        start_row, size = term_rows(s, chunk)
        rows = pl.ds(start_row, size)

        def body(j, carry):
            at = (role - 1) * blocks + j
            out_terms[s, at, rows] = out_terms[s, at, rows] + in_terms[s, (other - 1) * blocks + j, rows]
            return carry

        lax.fori_loop(0, blocks, body, 0, unroll=2 * UNROLL)

    def field_stage(s, chunk):
        field, term = copies(s, chunk)
        start(always, field[FACE])
        start(always, field[PAIR])

    def term_stage(s, chunk):
        field, term = copies(s, chunk)
        start_row, size = term_rows(s, chunk)
        with_ones = size > part
        rows = pl.ds(start_row, size)

        if with_ones:
            loads[1].wait()

        def row_body(i, carry):
            own = ext[s][chunk][i]
            pieces = split_parts(own)
            if with_ones:
                pieces.append(jnp.ones((16, own.shape[1]), jnp.bfloat16))
            stacked = jnp.concatenate(pieces, axis=0)
            for k in range(slots):
                made = jnp.dot(stacked, weights_ref[i, k], preferred_element_type=f32)
                term_now = made[:part] + made[part : 2 * part]
                if with_ones:
                    term_now = jnp.concatenate([made[2 * part : 2 * part + 8], term_now], axis=0)
                at = i * slots + k
                sums[at, :size] = term_now
            return carry

        lax.fori_loop(0, blocks, row_body, 0, unroll=UNROLL)

        def run_body(at, carry):
            sums[at, :size] = sums[at, :size] + sums[before_ref[at], :size]
            return carry

        lax.fori_loop(0, terms, run_body, 0, unroll=2 * UNROLL)
        if with_ones:
            make_tables()
        for role in (SIDE, FAR, PAIR, FACE):

            def pick(j, carry, role=role):
                out_terms[s, (role - 1) * blocks + j, rows] = sums[last_ref[role * blocks + j], :size]
                return carry

            lax.fori_loop(0, blocks, pick, 0, unroll=2 * UNROLL)
            if role == SIDE:
                start(jnp.logical_not(same) | has_src, term[SIDE])
            if role == FAR:
                start(same & has_src, term[FAR])
            if role == PAIR:
                start(always, term[PAIR])

        def keep(j, carry):
            kept[s, j, rows] = sums[last_ref[j], :size]
            return carry

        lax.fori_loop(0, blocks, keep, 0, unroll=2 * UNROLL)

    def far_terms_stage(s, chunk):
        field, term = copies(s, chunk)
        moved = jnp.logical_not(same) & has_src
        arrived(same | has_src, term[SIDE])

        @pl.when(moved)
        def _():
            add_terms(s, chunk, FAR, SIDE)

        start(moved, term[FAR])

    def face_relay_stage(s, chunk):
        field, term = copies(s, chunk)
        arrived(always, field[FACE])
        start(has_dst, field[FAR])
        start(same, field[SIDE])

    def face_terms_stage(s, chunk):
        field, term = copies(s, chunk)

        @pl.when(same)
        def _():
            add_terms(s, chunk, FACE, SIDE)

        arrived(has_dst, term[FAR])

        @pl.when(has_dst)
        def _():
            add_terms(s, chunk, FACE, FAR)

        start(always, term[FACE])

    def far_relay_stage(s, chunk):
        field, term = copies(s, chunk)
        arrived(has_src, field[FAR])
        start(jnp.logical_not(same) & has_src, field["other"])

    def forward_stage(s, chunk):
        field, term = copies(s, chunk)
        with_ones = s == 0 and chunk == 0
        here = pl.ds(chunk * part, part)
        arrived(always, field[PAIR])
        arrived(jnp.logical_not(same) | has_src, field[SIDE])

        def row_body(i, carry):
            made = None
            for k in range(slots):
                pieces = split_parts(ext[s][chunk][table_ref[cols_ref[i, k]]])
                if with_ones:
                    pieces.append(jnp.ones((16, width), jnp.bfloat16))
                stacked = jnp.concatenate(pieces, axis=0)
                product = lax.dot_general(
                    stacked, weights_ref[i, k], (((1,), (1,)), ((), ())), preferred_element_type=f32
                )
                made = product if made is None else made + product
            if with_ones:
                diag[i] = made[2 * part : 2 * part + 8] + prior_ref[pl.ds(i, 1), :]
            forward[i, here] = made[:part] + made[part : 2 * part]
            return carry

        lax.fori_loop(0, blocks, row_body, 0, unroll=UNROLL)

    def finish_stage(s, chunk):
        field, term = copies(s, chunk)
        start_row, size = term_rows(s, chunk)
        with_ones = size > part
        here = pl.ds(chunk * part, part)
        arrived(always, term[PAIR])
        arrived(always, term[FACE])

        def row_body(i, carry):
            trows = pl.ds(start_row, size)
            returned = (
                kept[s, i, trows]
                + in_terms[s, (PAIR - 1) * blocks + i, trows]
                + in_terms[s, (FACE - 1) * blocks + i, trows]
            )
            if with_ones:
                diag[i] = diag[i] + returned[:8]
                returned = returned[8:]
            coupled = forward[i, here] + returned
            now = ext[s][chunk][i]
            if chunk == 0:
                earlier = jnp.concatenate([now[:1], now[:-1]], axis=0)
            else:
                earlier = jnp.concatenate([ext[s][chunk - 1][i, part - 1 : part], now[:-1]], axis=0)
            if chunk == CHUNKS - 1:
                later = jnp.concatenate([now[1:], now[-1:]], axis=0)
            else:
                later = jnp.concatenate([now[1:], ext[s][chunk + 1][i, 0:1]], axis=0)
            diagonal = mask_f[i, here, :] + diag[i][:1]
            image = diagonal * now - coupled + time_tie * (2.0 * now - earlier - later)
            if s == 0:
                ext[1][chunk][i] = right[i, here, :] - image
            elif s == 1:
                ext[2][chunk][i] = image
                return (carry[0] + fold_rows(now * now), carry[1] + fold_rows(now * image))
            else:
                final[i, here, :] = image
            return carry

        zero = jnp.zeros((8, width), f32)
        return lax.fori_loop(0, blocks, row_body, (zero, zero), unroll=UNROLL)

    def reduce_start(index, tiles):
        for n, tile in enumerate(tiles):
            red_out[index, n] = tile
        sent = []
        for step in range(1, count):
            copy = pltpu.make_async_remote_copy(
                src_ref=red_out.at[index],
                dst_ref=red_in.at[index, step - 1],
                send_sem=red_send_sem.at[index],
                recv_sem=red_recv_sem.at[index],
                device_id={"graph": lax.rem(me + step, count)},
                device_id_type=MESH,
            )
            copy.start()

    def reduce_done(index, used):
        pltpu.make_async_copy(red_in.at[index], red_in.at[index], red_recv_sem.at[index]).wait()
        pltpu.make_async_copy(red_in.at[index], red_in.at[index], red_send_sem.at[index]).wait()
        values = []
        for n in range(used):
            tile = red_out[index, n]
            for step in range(1, count):
                tile = tile + red_in[index, step - 1, n]
            values.append(total_of(tile))
        return values

    def relay(s, chunk):
        far_terms_stage(s, chunk)
        face_relay_stage(s, chunk)
        face_terms_stage(s, chunk)
        far_relay_stage(s, chunk)

    zero = jnp.zeros((8, width), f32)
    for chunk in range(CHUNKS):
        field_stage(0, chunk)
    for chunk in range(CHUNKS):
        term_stage(0, chunk)
        far_terms_stage(0, chunk)
    for load in loads[2:]:
        load.wait()
    for i in range(blocks):
        seen = mask_ref[:, i, :].astype(f32)
        mask_f[i] = seen
        right[i] = seen * observed_ref[:, i, :]
    for s in range(APPLIED):
        for chunk in range(CHUNKS):
            face_relay_stage(s, chunk)
        if s == 2:
            norm_first, energy = reduce_done(0, 2)
            step_first = norm_first / energy

            def next_residual(i, carry):
                for chunk in range(CHUNKS):
                    fresh = ext[1][chunk][i] - step_first * ext[2][chunk][i]
                    right[i, pl.ds(chunk * part, part)] = fresh
                    carry = carry + fold_rows(fresh * fresh)
                return carry

            reduce_start(1, [lax.fori_loop(0, blocks, next_residual, zero)])
        for chunk in range(CHUNKS):
            face_terms_stage(s, chunk)
            far_relay_stage(s, chunk)
            if chunk == 0:
                forward_stage(s, chunk)
        dots = [zero, zero]
        for chunk in range(CHUNKS):
            if chunk > 0:
                forward_stage(s, chunk)
            made = finish_stage(s, chunk)
            dots = [dots[0] + made[0], dots[1] + made[1]]
            if s + 1 < APPLIED:
                field_stage(s + 1, chunk)
                if s == 1 and chunk == CHUNKS - 1:
                    reduce_start(0, dots)
                term_stage(s + 1, chunk)
                far_terms_stage(s + 1, chunk)
    (norm_second,) = reduce_done(1, 1)
    ratio = norm_second / norm_first

    def last_dot(i, carry):
        for chunk in range(CHUNKS):
            here = pl.ds(chunk * part, part)
            image = (1.0 + ratio) * ext[2][chunk][i] - step_first * final[i, here]
            direction = right[i, here] + ratio * ext[1][chunk][i]
            final[i, here] = image
            carry = carry + fold_rows(direction * image)
        return carry

    reduce_start(2, [lax.fori_loop(0, blocks, last_dot, zero)])
    (energy_second,) = reduce_done(2, 1)
    step_second = norm_second / energy_second
    for i in range(blocks):
        for chunk in range(CHUNKS):
            here = slice(chunk * part, (chunk + 1) * part)
            first = ext[1][chunk][i]
            fresh = right[i, here]
            direction = fresh + ratio * first
            solution_ref[here, i, :] = (ext[0][chunk][i] + step_first * first) + step_second * direction
            residual_ref[here, i, :] = fresh - step_second * final[i, here]
    for cond, copy in pending:
        pl.when(cond)(copy.wait_send)


def index_tables(block_cols, ext_count):
    flat = block_cols.reshape(-1)
    terms = flat.shape[0]
    order = jnp.arange(terms, dtype=jnp.int32)
    match = (flat[None, :] == flat[:, None]) & (order[None, :] < order[:, None])
    before = jnp.max(jnp.where(match, order[None, :], -1), axis=1)
    hits = flat[None, :] == jnp.arange(ext_count, dtype=jnp.int32)[:, None]
    last = jnp.max(jnp.where(hits, order[None, :], -1), axis=1)
    return jnp.where(before < 0, terms, before), jnp.where(last < 0, terms, last)


def per_device(count, observed, mask, first_guess, diag_weight, coupling, block_cols, send_rows):
    steps, blocks, width = observed.shape
    slots = coupling.shape[1]
    terms = blocks * slots
    part = steps // CHUNKS
    ext_count = blocks + 4 * send_rows.shape[2]
    before, last = index_tables(block_cols, ext_count)
    f32 = jnp.float32
    vmem = pl.BlockSpec(memory_space=pltpu.VMEM)
    smem = pl.BlockSpec(memory_space=pltpu.SMEM)
    shape = jax.ShapeDtypeStruct((steps, blocks, width), f32)
    return pl.pallas_call(
        functools.partial(cg_kernel, count, blocks, slots, steps),
        out_shape=(shape, shape),
        in_specs=[smem] * 3 + [pl.BlockSpec(memory_space=pl.ANY)] * 6,
        out_specs=(vmem, vmem),
        scratch_shapes=[pltpu.VMEM((5 * blocks, part, width), f32)] * (APPLIED * CHUNKS)
        + [
            pltpu.VMEM((blocks, steps, width), f32),
            pltpu.VMEM((blocks, steps, width), f32),
            pltpu.VMEM((blocks, steps, width), f32),
            pltpu.VMEM((blocks, steps, width), f32),
            pltpu.VMEM((terms + 1, part + 8, width), f32),
            pltpu.VMEM((APPLIED, blocks, steps + 8, width), f32),
            pltpu.VMEM((APPLIED, 4 * blocks, steps + 8, width), f32),
            pltpu.VMEM((APPLIED, 4 * blocks, steps + 8, width), f32),
            pltpu.VMEM((blocks, 8, width), f32),
            pltpu.VMEM((3, 2, 8, width), f32),
            pltpu.VMEM((3, count - 1, 2, 8, width), f32),
            pltpu.VMEM(observed.shape, f32),
            pltpu.VMEM(mask.shape, mask.dtype),
            pltpu.VMEM(first_guess.shape, f32),
            pltpu.VMEM(diag_weight.shape, f32),
            pltpu.VMEM(coupling.shape, coupling.dtype),
            pltpu.VMEM((4,) + send_rows.shape, jnp.int32),
            pltpu.SMEM((4,) + send_rows.shape, jnp.int32),
            pltpu.SMEM((ext_count,), jnp.int32),
            pltpu.SMEM((5 * blocks,), jnp.int32),
            pltpu.SemaphoreType.DMA((APPLIED, CHUNKS, 8)),
            pltpu.SemaphoreType.DMA((APPLIED, CHUNKS, 8)),
            pltpu.SemaphoreType.DMA((3,)),
            pltpu.SemaphoreType.DMA((3,)),
            pltpu.SemaphoreType.DMA((14,)),
        ],
        compiler_params=pltpu.CompilerParams(
            collective_id=0, has_side_effects=True, vmem_limit_bytes=LIMIT * 1024 * 1024
        ),
    )(before, last, block_cols, observed, mask, first_guess, diag_weight, coupling, send_rows)


def solution(mesh):
    fields = P(None, ("region", "graph"), None)
    placed = (
        fields,
        fields,
        fields,
        P(("region", "graph"), None),
        P(("region", "graph"), None, None, None),
        P(("region", "graph"), None),
        P(("region", "graph"), None, None),
    )
    return jax.shard_map(
        functools.partial(per_device, mesh.shape["graph"]),
        mesh=mesh,
        in_specs=placed,
        out_specs=(fields, fields),
        check_vma=False,
    )
```
